512 devices in a mesh: row: 32 (over x, y, core), col: 16 (over z).
Axes of the slice: x: 4, y: 4, z: 16, core: 2. Of those that a mesh axis runs over, the one named last changes fastest.
Arguments:
- inputs: bfloat16 [512, 16384], P('col', 'row'), may hold values from -6 to 6
- out_grad: bfloat16 [512, 16384], P('col', 'row'), may hold values from -6 to 6
- gate_weight: bfloat16 [16384, 13312], P('row', 'col'), may hold values from -0.046875 to 0.046875
- up_weight: bfloat16 [16384, 13312], P('row', 'col'), may hold values from -0.046875 to 0.046875
- down_weight: bfloat16 [13312, 16384], P('col', 'row'), may hold values from -0.0546875 to 0.0546875
Outputs:
- input_grad: bfloat16 [512, 16384], P('col', 'row')
- gate_grad: bfloat16 [16384, 13312], P('row', 'col')
- up_grad: bfloat16 [16384, 13312], P('row', 'col')
- down_grad: bfloat16 [13312, 16384], P('col', 'row')
The draws below stay inside these ranges and needn't reach their ends.
All inputs are finite; a program needn't handle non-finite values.
Results may differ from the reference program's by a relative error of at most 0.0049.
Values may be sent and summed in bfloat16 or wider, within the bound.
No kernel may reach another device: no remote copies, remote signals or barrier semaphores. Data moves between devices by JAX's collectives and lax.ppermute only.
A program may use at most 64 MiB of HBM per device.

```python
import jax
import jax.numpy as jnp
from jax import lax

D = 16384
FF = 13312
TOKENS = 512


def block_levels(stream_key, shape, pieces, smallest, top_value):
    gain = 1.0
    for dim, parts in pieces:
        draws = jax.random.uniform(jax.random.fold_in(jax.random.fold_in(stream_key, 6), dim), (parts,), jnp.float32, smallest / len(pieces), top_value / len(pieces))
        gain = gain * jnp.repeat(jnp.exp(draws), shape[dim] // parts).reshape((-1,) + (1,) * (len(shape) - 1 - dim))
    return gain


def gaussian(stream_key, shape, scale, most, cuts=(), kind=jnp.bfloat16):
    array = scale * jax.random.normal(stream_key, shape, jnp.float32)
    if cuts:
        array = array * block_levels(stream_key, shape, cuts, -0.22, 0.18)
    return jnp.clip(array, -most, most).astype(kind)


def setup_inputs(seed: int = 0) -> dict:
    splits = jax.random.split(jax.random.key(seed), 6)
    inputs = gaussian(splits[0], (TOKENS, D), 1.0, 6.0, ((0, 16), (1, 32)))
    out_grad = gaussian(splits[1], (TOKENS, D), 1.0, 6.0, ((0, 16), (1, 32)))
    gate_weight = gaussian(splits[2], (D, FF), D ** -0.5, 0.046875, ((0, 32), (1, 16)))
    up_weight = gaussian(splits[3], (D, FF), D ** -0.5, 0.046875, ((0, 32), (1, 16)))
    down_weight = gaussian(splits[4], (FF, D), FF ** -0.5, 0.0546875, ((0, 16), (1, 32)))
    return dict(inputs=inputs, out_grad=out_grad, gate_weight=gate_weight, up_weight=up_weight, down_weight=down_weight)


def reference(inputs, out_grad, gate_weight, up_weight, down_weight):
    gate = jnp.dot(inputs, gate_weight, preferred_element_type=jnp.float32)
    up = jnp.dot(inputs, up_weight, preferred_element_type=jnp.float32)
    hidden_grad = lax.dot_general(out_grad, down_weight, (((1,), (1,)), ((), ())), preferred_element_type=jnp.float32)
    sig = jax.nn.sigmoid(gate)
    silu = gate * sig
    hidden = (silu * up).astype(jnp.bfloat16)
    gate_delta = (hidden_grad * up * sig * (1.0 + gate * (1.0 - sig))).astype(jnp.bfloat16)
    up_delta = (hidden_grad * silu).astype(jnp.bfloat16)
    down_grad = lax.dot_general(hidden, out_grad, (((0,), (0,)), ((), ())), preferred_element_type=jnp.float32).astype(jnp.bfloat16)
    gate_grad = lax.dot_general(inputs, gate_delta, (((0,), (0,)), ((), ())), preferred_element_type=jnp.float32).astype(jnp.bfloat16)
    up_grad = lax.dot_general(inputs, up_delta, (((0,), (0,)), ((), ())), preferred_element_type=jnp.float32).astype(jnp.bfloat16)
    input_grad = lax.dot_general(gate_delta, gate_weight, (((1,), (1,)), ((), ())), preferred_element_type=jnp.float32)
    input_grad = input_grad + lax.dot_general(up_delta, up_weight, (((1,), (1,)), ((), ())), preferred_element_type=jnp.float32)
    return input_grad.astype(jnp.bfloat16), gate_grad, up_grad, down_grad
```

```python
import jax
import jax.numpy as jnp
from jax import lax
from jax.sharding import Mesh, PartitionSpec as P

BF16, F32 = jnp.bfloat16, jnp.float32
XY = ("x", "y")


def nonlinear(gate, up, hidden_grad):
    sig = jax.nn.sigmoid(gate)
    silu = gate * sig
    hidden = (silu * up).astype(BF16)
    gate_delta = (hidden_grad * up * sig * (1.0 + gate * (1.0 - sig))).astype(BF16)
    up_delta = (hidden_grad * silu).astype(BF16)
    return (hidden, gate_delta, up_delta)


def contract(left, right, left_dim, right_dim):
    return lax.dot_general(
        left, right, (((left_dim,), (right_dim,)), ((), ())), preferred_element_type=F32
    )


def spread(block, axes, n):
    return lax.all_to_all(jnp.broadcast_to(block, (n, *block.shape)), axes, 0, 0)


def swap_cores(value):
    return jax.tree.map(lambda v: lax.ppermute(v, "core", [(0, 1), (1, 0)]), value)


def per_device(inputs, out_grad, gate_weight, up_weight, down_weight):
    tokens, width = inputs.shape
    hidden_units = gate_weight.shape[1]
    core = lax.axis_index("core")
    both = jnp.stack([inputs, out_grad])
    near = spread(both, "z_hi", 4)
    every = spread(near, "z_lo", 4)
    half = 8 * tokens
    halves = every.transpose(2, 0, 1, 3, 4).reshape(2, 2, half, width)

    def pick(which):
        part = lax.dynamic_index_in_dim(halves, which, 1, keepdims=False)
        return part[0], part[1]

    x_own, g_own = pick(core)
    x_other, g_other = pick(1 - core)

    def products(x, g):
        return (
            jnp.dot(x, gate_weight, preferred_element_type=F32),
            jnp.dot(x, up_weight, preferred_element_type=F32),
            contract(g, down_weight, 1, 1),
        )

    arrived = swap_cores(products(x_other, g_other))
    sums = [(a + b).astype(BF16) for a, b in zip(products(x_own, g_own), arrived, strict=True)]
    n = 16
    parts = jnp.stack([s.reshape(n, half // n, hidden_units) for s in sums], axis=1)
    parts = lax.all_to_all(parts, XY, 0, 0)
    total = jnp.sum(parts.astype(F32), axis=0)
    result = jnp.stack(nonlinear(total[0], total[1], total[2]))
    own = spread(result, XY, n)
    own = own.transpose(1, 0, 2, 3).reshape(3, half, hidden_units)
    other = swap_cores(own)

    def input_part(deltas):
        return contract(deltas[1], gate_weight, 1, 1) + contract(deltas[2], up_weight, 1, 1)

    grads_in = jnp.zeros((2, half, width), BF16)
    for which, deltas in ((core, own), (1 - core, other)):
        grads_in = lax.dynamic_update_index_in_dim(
            grads_in, input_part(deltas).astype(BF16), which, 0
        )
    pieces = lax.all_to_all(grads_in.reshape(16, tokens, width), ("z_lo", "z_hi"), 0, 0)
    input_grad = jnp.sum(pieces.astype(F32), axis=0).astype(BF16)

    down_grad = contract(own[0], g_own, 0, 0) + contract(other[0], g_other, 0, 0)
    gate_grad = contract(x_own, own[1], 0, 0) + contract(x_other, other[1], 0, 0)
    up_grad = contract(x_own, own[2], 0, 0) + contract(x_other, other[2], 0, 0)
    return (input_grad, gate_grad.astype(BF16), up_grad.astype(BF16), down_grad.astype(BF16))


def solution(mesh):
    grid = Mesh(
        mesh.devices.reshape(4, 4, 2, 4, 4), ("x", "y", "core", "z_hi", "z_lo")
    )
    row, col = ("x", "y", "core"), ("z_hi", "z_lo")
    return jax.shard_map(
        per_device,
        mesh=grid,
        in_specs=(P(col, row), P(col, row), P(row, col), P(row, col), P(col, row)),
        out_specs=(P(col, row), P(row, col), P(row, col), P(col, row)),
        check_vma=False,
    )
```

```python
import functools

import jax
import jax.numpy as jnp
from jax import lax
from jax.experimental import pallas as pl
from jax.experimental.pallas import tpu as pltpu
from jax.sharding import Mesh, PartitionSpec as P

BF16, F32 = jnp.bfloat16, jnp.float32
XY = ("x", "y")
FAR = 4
OFFSETS = (0, 1, -1, 2)
VMEM = pl.BlockSpec(memory_space=pltpu.VMEM)
SMEM = pl.BlockSpec(memory_space=pltpu.SMEM)


def nonlinear(gate, up, hidden_grad):
    sig = jax.nn.sigmoid(gate)
    silu = gate * sig
    hidden = (silu * up).astype(BF16)
    gate_delta = (hidden_grad * up * sig * (1.0 + gate * (1.0 - sig))).astype(BF16)
    up_delta = (hidden_grad * silu).astype(BF16)
    return (hidden, gate_delta, up_delta)


def contract(left, right, left_dim, right_dim):
    return lax.dot_general(
        left, right, (((left_dim,), (right_dim,)), ((), ())), preferred_element_type=F32
    )


def call(body, outs, flops, *args):
    moved = sum(a.size * a.dtype.itemsize for a in (*args, *jax.tree.leaves(outs)))
    return pl.pallas_call(
        body,
        out_shape=outs,
        in_specs=[SMEM if a.dtype == jnp.int32 else VMEM for a in args],
        out_specs=jax.tree.map(lambda _: VMEM, outs),
        compiler_params=pltpu.CompilerParams(vmem_limit_bytes=28 * 2**20),
        cost_estimate=pl.CostEstimate(flops=flops, bytes_accessed=moved, transcendentals=0),
    )(*args)


def half_rows(which, kind, near, second_low, second_high):
    rows = []
    for far in range(2):
        rows += [ref[2 * which + far, kind] for ref in near]
        rows.append(jnp.where(which == 0, second_low[far, kind], second_high[far, kind]))
    return jnp.concatenate(rows, 0)


def send_body(kind, where, a, b, c, d, e, weight, out):
    rows = half_rows(1 - where[0], kind, (a, b, c), d, e)
    out[...] = contract(rows, weight[...], 1, 1).reshape(out.shape)


def keep_body(where, a, b, c, d, e, pair, down, got_pair, got_down, out):
    blocks, rows, _ = out.shape
    wide = pair.shape[0]
    for kind, weight, got, lanes in (
        (0, pair, got_pair, slice(0, wide)),
        (1, down, got_down, slice(wide, None)),
    ):
        mine = half_rows(where[0], kind, (a, b, c), d, e)
        total = contract(mine, weight[...], 1, 1).reshape(blocks, rows, -1)
        out[:, :, lanes] = (total + got[...]).astype(BF16)


def middle_body(parts, out):
    units = parts.shape[2] // 3
    total = parts[0].astype(F32)
    for i in range(1, parts.shape[0]):
        total += parts[i].astype(F32)
    hid, gate_delta, up_delta = nonlinear(
        total[:, :units], total[:, units : 2 * units], total[:, 2 * units :]
    )
    row = jnp.concatenate([gate_delta, up_delta, hid], 1)
    out[...] = jnp.broadcast_to(row[None], out.shape)


def own_body(deltas, pair, out):
    out[...] = contract(deltas[:, : pair.shape[0]], pair[...], 1, 0).astype(BF16)


def other_body(where, deltas, pair, own, out):
    other = contract(deltas[:, : pair.shape[0]], pair[...], 1, 0).astype(BF16)
    tokens = out.shape[2]
    mine = own[...]
    for far in range(2):
        for k, offset in enumerate(OFFSETS):
            start = (far * FAR + k) * tokens
            group = lax.rem(where[1] + FAR + offset, FAR)
            out[2 * where[0] + far, group] = mine[start : start + tokens]
            out[2 * (1 - where[0]) + far, group] = other[start : start + tokens]


def swap_cores(value):
    return lax.ppermute(value, "core", [(0, 1), (1, 0)])


def shift(value, by):
    return lax.ppermute(value, "col", [((i + by) % 16, i) for i in range(16)])


def per_device(inputs, out_grad, gate_weight, up_weight, down_weight):
    tokens, width = inputs.shape
    units = gate_weight.shape[1]
    n = 16
    half = n * tokens // 2
    core, col = lax.axis_index("core"), lax.axis_index("col")
    where = jnp.stack([core, lax.rem(col, FAR)]).astype(jnp.int32)
    pair = jnp.concatenate([gate_weight.T, up_weight.T], 0)

    both = jnp.stack([inputs, out_grad])
    apart = [[r + FAR * i for i in range(FAR)] for r in range(FAR)]
    first = lax.all_to_all(
        jnp.broadcast_to(both, (FAR, *both.shape)), "col", 0, 0, axis_index_groups=apart
    )
    after, before = shift(first, 1), shift(first, -1)
    low, high = shift(first[:2], 2), shift(first[2:], -2)
    held = (first, after, before, low, high)

    flops = 2 * half * units * width
    sds = jax.ShapeDtypeStruct
    sent = [
        swap_cores(
            call(
                functools.partial(send_body, kind),
                sds((n, half // n, weight.shape[0]), F32),
                flops * (2 - kind),
                where,
                *held,
                weight,
            )
        )
        for kind, weight in ((0, pair), (1, down_weight))
    ]
    parts = call(
        keep_body, sds((n, half // n, 3 * units), BF16), 3 * flops, where, *held, pair, down_weight, *sent
    )
    parts = lax.all_to_all(parts, XY, 0, 0)
    row = call(middle_body, sds(parts.shape, BF16), 40 * half // n * units, parts)
    row = lax.all_to_all(row, XY, 0, 0).reshape(half, 3 * units)
    other = swap_cores(row)
    own_part = call(own_body, sds((half, width), BF16), 2 * flops, row, pair)
    pieces = call(
        other_body, sds((FAR, FAR, tokens, width), BF16), 2 * flops, where, other, pair, own_part
    )
    pieces = lax.all_to_all(pieces.reshape(n, tokens, width), "col", 0, 0)
    input_grad = jnp.sum(pieces.astype(F32), axis=0).astype(BF16)

    def ordered(kind):
        last = jnp.concatenate([low, high], 0)
        groups = [g[:, kind] for g in (first, after, before, last)]
        return jnp.stack(groups, axis=1).reshape(2 * half, width)

    def grad(lanes, value):
        total = contract(row[:, lanes], lax.dynamic_slice_in_dim(value, core * half, half, 0), 0, 0)
        others = lax.dynamic_slice_in_dim(value, (1 - core) * half, half, 0)
        rest = contract(other[:, lanes], others, 0, 0)
        return (total + rest).astype(BF16)

    pair_grad = grad(slice(0, 2 * units), ordered(0))
    down_grad = grad(slice(2 * units, None), ordered(1))
    return (input_grad, pair_grad[:units].T, pair_grad[units:].T, down_grad)


def solution(mesh):
    grid = Mesh(mesh.devices.reshape(4, 4, 2, 16), ("x", "y", "core", "col"))
    row = ("x", "y", "core")
    return jax.shard_map(
        per_device,
        mesh=grid,
        in_specs=(P("col", row), P("col", row), P(row, "col"), P(row, "col"), P("col", row)),
        out_specs=(P("col", row), P(row, "col"), P(row, "col"), P("col", row)),
        check_vma=False,
    )
```

```python
import jax
import jax.numpy as jnp
from jax import lax
from jax.experimental import pallas as pl
from jax.experimental.pallas import tpu as pltpu
from jax.sharding import Mesh, PartitionSpec as P

BF16, F32 = jnp.bfloat16, jnp.float32
XY = ("x", "y")
VMEM = pl.BlockSpec(memory_space=pltpu.VMEM)
SMEM = pl.BlockSpec(memory_space=pltpu.SMEM)


def nonlinear(gate, up, hidden_grad):
    sig = jax.nn.sigmoid(gate)
    silu = gate * sig
    hidden = (silu * up).astype(BF16)
    gate_delta = (hidden_grad * up * sig * (1.0 + gate * (1.0 - sig))).astype(BF16)
    up_delta = (hidden_grad * silu).astype(BF16)
    return (hidden, gate_delta, up_delta)


def contract(left, right, left_dim, right_dim):
    return lax.dot_general(
        left, right, (((left_dim,), (right_dim,)), ((), ())), preferred_element_type=F32
    )


def call(body, outs, flops, *args):
    moved = sum(a.size * a.dtype.itemsize for a in (*args, *jax.tree.leaves(outs)))
    return pl.pallas_call(
        body,
        out_shape=outs,
        in_specs=[SMEM if a.dtype == jnp.int32 else VMEM for a in args],
        out_specs=jax.tree.map(lambda _: VMEM, outs),
        compiler_params=pltpu.CompilerParams(vmem_limit_bytes=28 * 2**20),
        cost_estimate=pl.CostEstimate(flops=flops, bytes_accessed=moved, transcendentals=0),
    )(*args)


def half_inputs(which, first):
    devices, tokens = first.shape[0] // 2, 32
    return first[pl.ds(which * devices, devices), :tokens].reshape(devices * tokens, -1)


def half_grads(which, first, second):
    devices = first.shape[0] // 2
    span = pl.ds(which * devices, devices)
    rows = jnp.concatenate([first[span, 32:], second[span]], 1)
    return rows.reshape(devices * 32, -1)


def send_x_body(where, first, weight, out, rows_out):
    rows = half_inputs(1 - where[0], first)
    rows_out[...] = rows
    out[...] = contract(rows, weight[...], 1, 1).reshape(out.shape)


def send_g_body(where, first, second, weight, out, rows_out):
    rows = half_grads(1 - where[0], first, second)
    rows_out[...] = rows
    out[...] = contract(rows, weight[...], 1, 1).reshape(out.shape)


def keep_body(where, first, second, pair, down, got_pair, got_down, out, x_out, g_out):
    blocks, rows, _ = out.shape
    wide = pair.shape[0]
    mine = half_inputs(where[0], first)
    x_out[...] = mine
    total = contract(mine, pair[...], 1, 1).reshape(blocks, rows, -1)
    out[:, :, :wide] = (total + got_pair[...]).astype(BF16)
    mine = half_grads(where[0], first, second)
    g_out[...] = mine
    total = contract(mine, down[...], 1, 1).reshape(blocks, rows, -1)
    out[:, :, wide:] = (total + got_down[...]).astype(BF16)


def middle_body(parts, deltas, hidden):
    units = parts.shape[2] // 3
    total = parts[0].astype(F32)
    for i in range(1, parts.shape[0]):
        total += parts[i].astype(F32)
    hid, gate_delta, up_delta = nonlinear(
        total[:, :units], total[:, units : 2 * units], total[:, 2 * units :]
    )
    hidden[...] = hid
    row = jnp.concatenate([gate_delta, up_delta], 1)
    deltas[...] = jnp.broadcast_to(row[None], deltas.shape)


def part_of(deltas, pair):
    lanes = pair.shape[0]
    rows = deltas[...].reshape(-1, deltas.shape[-1])[:, :lanes]
    return contract(rows, pair[...], 1, 0).astype(BF16)


def own_body(deltas, pair, out):
    out[...] = part_of(deltas, pair)


def other_body(where, deltas, pair, own, out):
    out[where[0]] = own[...]
    out[1 - where[0]] = part_of(deltas, pair)


def swap_cores(value):
    return lax.ppermute(value, "core", [(0, 1), (1, 0)])


def per_device(inputs, out_grad, gate_weight, up_weight, down_weight):
    tokens, width = inputs.shape
    units = gate_weight.shape[1]
    n = 16
    half = n * tokens // 2
    core = lax.axis_index("core")
    where = core.astype(jnp.int32).reshape(1)
    pair = jnp.concatenate([gate_weight.T, up_weight.T], 0)

    early = tokens // 2
    second = lax.all_to_all(
        jnp.broadcast_to(out_grad[early:], (n, tokens - early, width)), "col", 0, 0
    )
    first = lax.all_gather(jnp.concatenate([inputs, out_grad[:early]], 0), "col", axis=0)

    flops = 2 * half * units * width
    sds = jax.ShapeDtypeStruct
    rows = sds((half, width), BF16)
    sent_x, x_other = call(
        send_x_body, (sds((n, half // n, 2 * units), F32), rows), 2 * flops, where, first, pair
    )
    got_x = swap_cores(sent_x)
    sent_g, g_other = call(
        send_g_body,
        (sds((n, half // n, units), F32), rows),
        flops,
        where,
        first,
        second,
        down_weight,
    )
    got_g = swap_cores(sent_g)
    parts, x_own, g_own = call(
        keep_body,
        (sds((n, half // n, 3 * units), BF16), rows, rows),
        3 * flops,
        where,
        first,
        second,
        pair,
        down_weight,
        got_x,
        got_g,
    )
    parts = lax.all_to_all(parts, XY, 0, 0)
    own, hidden = call(
        middle_body,
        (sds((n, half // n, 2 * units), BF16), sds((half // n, units), BF16)),
        40 * half // n * units,
        parts,
    )
    own = lax.all_to_all(own, XY, 0, 0)
    other = swap_cores(own)
    own_part = call(own_body, rows, 2 * flops, own, pair)
    pieces = call(
        other_body, sds((2, half, width), BF16), 2 * flops, where, other, pair, own_part
    )
    pieces = lax.all_to_all(pieces.reshape(n, tokens, width), "col", 0, 0)
    input_grad = jnp.sum(pieces.astype(F32), axis=0).astype(BF16)
    pair_grad = contract(own.reshape(half, -1), x_own, 0, 0)
    pair_grad = (pair_grad + contract(other.reshape(half, -1), x_other, 0, 0)).astype(BF16)
    hidden = lax.all_gather(hidden, ("x", "y", "core"), axis=0).reshape(n, 2, half // n, units)
    hidden_own = lax.dynamic_index_in_dim(hidden, core, 1, keepdims=False).reshape(half, units)
    hidden_other = lax.dynamic_index_in_dim(hidden, 1 - core, 1, keepdims=False)
    down_grad = contract(hidden_own, g_own, 0, 0)
    down_grad = down_grad + contract(hidden_other.reshape(half, units), g_other, 0, 0)
    return (input_grad, pair_grad[:units].T, pair_grad[units:].T, down_grad.astype(BF16))
def solution(mesh):
    grid = Mesh(mesh.devices.reshape(4, 4, 2, 16), ("x", "y", "core", "col"))
    row = ("x", "y", "core")
    return jax.shard_map(
        per_device,
        mesh=grid,
        in_specs=(P("col", row), P("col", row), P(row, "col"), P(row, "col"), P("col", row)),
        out_specs=(P("col", row), P(row, "col"), P(row, "col"), P("col", row)),
        check_vma=False,
    )
```

```python
import jax
import jax.numpy as jnp
from jax import lax
from jax.experimental import pallas as pl
from jax.experimental.pallas import tpu as pltpu
from jax.sharding import Mesh, PartitionSpec as P

BF16, F32 = jnp.bfloat16, jnp.float32
XY = ("x", "y")
FAR = 4
OFFSETS = (0, 1, -1, 2)
VMEM = pl.BlockSpec(memory_space=pltpu.VMEM)
SMEM = pl.BlockSpec(memory_space=pltpu.SMEM)


def nonlinear(gate, up, hidden_grad):
    sig = jax.nn.sigmoid(gate)
    silu = gate * sig
    hidden = (silu * up).astype(BF16)
    gate_delta = (hidden_grad * up * sig * (1.0 + gate * (1.0 - sig))).astype(BF16)
    up_delta = (hidden_grad * silu).astype(BF16)
    return (hidden, gate_delta, up_delta)


def contract(left, right, left_dim, right_dim):
    return lax.dot_general(
        left, right, (((left_dim,), (right_dim,)), ((), ())), preferred_element_type=F32
    )


def call(body, outs, flops, *args):
    moved = sum(a.size * a.dtype.itemsize for a in (*args, *jax.tree.leaves(outs)))
    return pl.pallas_call(
        body,
        out_shape=outs,
        in_specs=[SMEM if a.dtype == jnp.int32 else VMEM for a in args],
        out_specs=jax.tree.map(lambda _: VMEM, outs),
        compiler_params=pltpu.CompilerParams(vmem_limit_bytes=20 * 2**20),
        cost_estimate=pl.CostEstimate(flops=flops, bytes_accessed=moved, transcendentals=0),
    )(*args)


def half_rows(which, kind, near, second_low, second_high):
    rows = []
    for far in range(2):
        rows += [ref[2 * which + far, kind] for ref in near]
        rows.append(jnp.where(which == 0, second_low[far, kind], second_high[far, kind]))
    return jnp.concatenate(rows, 0)


def send_body(where, a, b, c, d, e, pair, down, pair_out, down_out):
    for kind, weight, out in ((0, pair, pair_out), (1, down, down_out)):
        rows = half_rows(1 - where[0], kind, (a, b, c), d, e)
        out[...] = contract(rows, weight[...], 1, 1).reshape(out.shape)


def keep_body(where, a, b, c, d, e, pair, down, got_pair, got_down, out):
    blocks, rows, _ = out.shape
    wide = pair.shape[0]
    for kind, weight, got, lanes in (
        (0, pair, got_pair, slice(0, wide)),
        (1, down, got_down, slice(wide, None)),
    ):
        mine = half_rows(where[0], kind, (a, b, c), d, e)
        total = contract(mine, weight[...], 1, 1).reshape(blocks, rows, -1)
        out[:, :, lanes] = (total + got[...]).astype(BF16)


def middle_body(parts, out):
    units = parts.shape[2] // 3
    total = parts[0].astype(F32)
    for i in range(1, parts.shape[0]):
        total += parts[i].astype(F32)
    hid, gate_delta, up_delta = nonlinear(
        total[:, :units], total[:, units : 2 * units], total[:, 2 * units :]
    )
    row = jnp.concatenate([gate_delta, up_delta, hid], 1)
    out[...] = jnp.broadcast_to(row[None], out.shape)


def part_of(deltas, pair):
    lanes = pair.shape[0]
    rows = deltas[...].reshape(-1, deltas.shape[-1])[:, :lanes]
    return contract(rows, pair[...], 1, 0).astype(BF16)


def own_body(deltas, pair, out):
    out[...] = part_of(deltas, pair)


def other_body(where, deltas, pair, own, out):
    devices, tokens, _ = out.shape
    parts = (own[...], part_of(deltas, pair))
    for far in range(2):
        for k, offset in enumerate(OFFSETS):
            start = (far * len(OFFSETS) + k) * tokens
            for half, part in zip((where[0], 1 - where[0]), parts, strict=True):
                device = lax.rem(where[1] + devices + offset + FAR * (2 * half + far), devices)
                out[device] = part[start : start + tokens]


def rows_body(where, a, b, c, d, e, _, x_own, g_own, x_other, g_other):
    for kind, own, other in ((0, x_own, x_other), (1, g_own, g_other)):
        own[...] = half_rows(where[0], kind, (a, b, c), d, e)
        other[...] = half_rows(1 - where[0], kind, (a, b, c), d, e)


def swap_cores(value):
    return lax.ppermute(value, "core", [(0, 1), (1, 0)])


def shift(value, by):
    return lax.ppermute(value, "col", [((i + by) % 16, i) for i in range(16)])


def per_device(inputs, out_grad, gate_weight, up_weight, down_weight):
    tokens, width = inputs.shape
    units = gate_weight.shape[1]
    n = 16
    half = n * tokens // 2
    core, col = lax.axis_index("core"), lax.axis_index("col")
    where = jnp.stack([core, col]).astype(jnp.int32)
    pair = jnp.concatenate([gate_weight.T, up_weight.T], 0)

    both = jnp.stack([inputs, out_grad])
    group = jnp.stack([both, shift(both, FAR), shift(both, 2 * FAR), shift(both, -FAR)])
    after, before = shift(group, 1), shift(group, -1)
    low = shift(group[:2], 2)
    high = shift(jnp.concatenate([group[3:], group[:1]]), -2)
    held = (group, after, before, low, high)

    flops = 2 * half * units * width
    sds = jax.ShapeDtypeStruct
    sent = call(
        send_body,
        (sds((n, half // n, 2 * units), F32), sds((n, half // n, units), F32)),
        3 * flops,
        where,
        *held,
        pair,
        down_weight,
    )
    sent = [swap_cores(value) for value in sent]
    parts = call(
        keep_body, sds((n, half // n, 3 * units), BF16), 3 * flops, where, *held, pair, down_weight, *sent
    )
    parts = lax.all_to_all(parts, XY, 0, 0)
    row = call(middle_body, sds(parts.shape, BF16), 40 * half // n * units, parts)
    own = lax.all_to_all(row, XY, 0, 0)
    other = swap_cores(own)
    rows = sds((half, width), BF16)
    own_part = call(own_body, rows, 2 * flops, own, pair)
    pieces = call(
        other_body, sds((n, tokens, width), BF16), 2 * flops, where, other, pair, own_part
    )
    x_own, g_own, x_other, g_other = call(rows_body, (rows,) * 4, 0, where, *held, pieces)
    pieces = lax.all_to_all(pieces, "col", 0, 0)
    input_grad = jnp.sum(pieces.astype(F32), axis=0).astype(BF16)

    def grad(lanes, mine, others):
        total = contract(own.reshape(half, -1)[:, lanes], mine, 0, 0)
        return (total + contract(other.reshape(half, -1)[:, lanes], others, 0, 0)).astype(BF16)

    pair_grad = grad(slice(0, 2 * units), x_own, x_other)
    down_grad = grad(slice(2 * units, None), g_own, g_other)
    return (input_grad, pair_grad[:units].T, pair_grad[units:].T, down_grad)


def solution(mesh):
    grid = Mesh(mesh.devices.reshape(4, 4, 2, 16), ("x", "y", "core", "col"))
    row = ("x", "y", "core")
    return jax.shard_map(
        per_device,
        mesh=grid,
        in_specs=(P("col", row), P("col", row), P(row, "col"), P(row, "col"), P("col", row)),
        out_specs=(P("col", row), P(row, "col"), P(row, "col"), P("col", row)),
        check_vma=False,
    )
```

```python
import jax
import jax.numpy as jnp
from jax import lax
from jax.experimental import pallas as pl
from jax.experimental.pallas import tpu as pltpu
from jax.sharding import Mesh, PartitionSpec as P

BF16, F32 = jnp.bfloat16, jnp.float32
XY = ("x", "y")
FAR = 4
OFFSETS = (0, 1, -1, 2)
VMEM = pl.BlockSpec(memory_space=pltpu.VMEM)
SMEM = pl.BlockSpec(memory_space=pltpu.SMEM)


def nonlinear(gate, up, hidden_grad):
    sig = jax.nn.sigmoid(gate)
    silu = gate * sig
    hidden = (silu * up).astype(BF16)
    gate_delta = (hidden_grad * up * sig * (1.0 + gate * (1.0 - sig))).astype(BF16)
    up_delta = (hidden_grad * silu).astype(BF16)
    return (hidden, gate_delta, up_delta)


def contract(left, right, left_dim, right_dim):
    return lax.dot_general(
        left, right, (((left_dim,), (right_dim,)), ((), ())), preferred_element_type=F32
    )


def call(body, outs, flops, *args):
    moved = sum(a.size * a.dtype.itemsize for a in (*args, *jax.tree.leaves(outs)))
    return pl.pallas_call(
        body,
        out_shape=outs,
        in_specs=[SMEM if a.dtype == jnp.int32 else VMEM for a in args],
        out_specs=jax.tree.map(lambda _: VMEM, outs),
        compiler_params=pltpu.CompilerParams(vmem_limit_bytes=32 * 2**20),
        cost_estimate=pl.CostEstimate(flops=flops, bytes_accessed=moved, transcendentals=0),
    )(*args)


def half_rows(which, kind, near, second_low, second_high):
    rows = []
    for far in range(2):
        rows += [ref[2 * which + far, kind] for ref in near]
        rows.append(jnp.where(which == 0, second_low[far, kind], second_high[far, kind]))
    return jnp.concatenate(rows, 0)


def send_body(where, a, b, c, d, e, pair, down, pair_out, down_out):
    for kind, weight, out in ((0, pair, pair_out), (1, down, down_out)):
        rows = half_rows(1 - where[0], kind, (a, b, c), d, e)
        out[...] = contract(rows, weight[...], 1, 1).reshape(out.shape)


def keep_body(where, a, b, c, d, e, pair, down, got_pair, got_down, out):
    blocks, rows, _ = out.shape
    wide = pair.shape[0]
    for kind, weight, got, lanes in (
        (0, pair, got_pair, slice(0, wide)),
        (1, down, got_down, slice(wide, None)),
    ):
        mine = half_rows(where[0], kind, (a, b, c), d, e)
        total = contract(mine, weight[...], 1, 1).reshape(blocks, rows, -1)
        out[:, :, lanes] = (total + got[...]).astype(BF16)


def middle_body(parts, out):
    units = parts.shape[2] // 3
    total = parts[0].astype(F32)
    for i in range(1, parts.shape[0]):
        total += parts[i].astype(F32)
    hid, gate_delta, up_delta = nonlinear(
        total[:, :units], total[:, units : 2 * units], total[:, 2 * units :]
    )
    row = jnp.concatenate([gate_delta, up_delta, hid], 1)
    out[...] = jnp.broadcast_to(row[None], out.shape)


def part_of(deltas, pair):
    lanes = pair.shape[0]
    rows = deltas[...].reshape(-1, deltas.shape[-1])[:, :lanes]
    return contract(rows, pair[...], 1, 0).astype(BF16)


def own_body(deltas, pair, out):
    out[...] = part_of(deltas, pair)


def other_body(where, deltas, pair, own, out):
    devices, tokens, _ = out.shape
    parts = (own[...], part_of(deltas, pair))
    for far in range(2):
        for k, offset in enumerate(OFFSETS):
            start = (far * len(OFFSETS) + k) * tokens
            for half, part in zip((where[0], 1 - where[0]), parts, strict=True):
                device = lax.rem(where[1] + devices + offset + FAR * (2 * half + far), devices)
                out[device] = part[start : start + tokens]


def grads_body(where, a, b, c, d, e, own, other, pieces, input_out, gate_out, up_out, down_out):
    total = pieces[0].astype(F32)
    for i in range(1, pieces.shape[0]):
        total += pieces[i].astype(F32)
    input_out[...] = total.astype(BF16)
    units = gate_out.shape[0]
    deltas = [ref[...].reshape(-1, ref.shape[-1]) for ref in (own, other)]

    def total_of(kind, lanes):
        halves = (where[0], 1 - where[0])
        rows = jnp.concatenate([half_rows(h, kind, (a, b, c), d, e) for h in halves], 0)
        return contract(jnp.concatenate([m[:, lanes] for m in deltas], 0), rows, 0, 0).astype(BF16)

    pair = total_of(0, slice(0, 2 * units))
    gate_out[...] = pair[:units]
    up_out[...] = pair[units:]
    down_out[...] = total_of(1, slice(2 * units, 3 * units))


def swap_cores(value):
    return lax.ppermute(value, "core", [(0, 1), (1, 0)])


def shift(value, by):
    return lax.ppermute(value, "col", [((i + by) % 16, i) for i in range(16)])


def per_device(inputs, out_grad, gate_weight, up_weight, down_weight):
    tokens, width = inputs.shape
    units = gate_weight.shape[1]
    n = 16
    half = n * tokens // 2
    core, col = lax.axis_index("core"), lax.axis_index("col")
    where = jnp.stack([core, col]).astype(jnp.int32)
    pair = jnp.concatenate([gate_weight.T, up_weight.T], 0)

    both = jnp.stack([inputs, out_grad])
    group = jnp.stack([both, shift(both, FAR), shift(both, 2 * FAR), shift(both, -FAR)])
    after, before = shift(group, 1), shift(group, -1)
    low = shift(group[:2], 2)
    high = shift(jnp.concatenate([group[3:], group[:1]]), -2)
    held = (group, after, before, low, high)

    flops = 2 * half * units * width
    sds = jax.ShapeDtypeStruct
    sent = call(
        send_body,
        (sds((n, half // n, 2 * units), F32), sds((n, half // n, units), F32)),
        3 * flops,
        where,
        *held,
        pair,
        down_weight,
    )
    sent = [swap_cores(value) for value in sent]
    parts = call(
        keep_body, sds((n, half // n, 3 * units), BF16), 3 * flops, where, *held, pair, down_weight, *sent
    )
    parts = lax.all_to_all(parts, XY, 0, 0)
    row = call(middle_body, sds(parts.shape, BF16), 40 * half // n * units, parts)
    own = lax.all_to_all(row, XY, 0, 0)
    other = swap_cores(own)
    own_part = call(own_body, sds((half, width), BF16), 2 * flops, own, pair)
    pieces = call(
        other_body, sds((n, tokens, width), BF16), 2 * flops, where, other, pair, own_part
    )
    pieces = lax.all_to_all(pieces, "col", 0, 0)
    grad = sds((units, width), BF16)
    input_grad, gate_grad, up_grad, down_grad = call(
        grads_body,
        (sds((tokens, width), BF16), grad, grad, grad),
        6 * flops,
        where,
        *held,
        own,
        other,
        pieces,
    )
    return (input_grad, gate_grad.T, up_grad.T, down_grad)


def solution(mesh):
    grid = Mesh(mesh.devices.reshape(4, 4, 2, 16), ("x", "y", "core", "col"))
    row = ("x", "y", "core")
    return jax.shard_map(
        per_device,
        mesh=grid,
        in_specs=(P("col", row), P("col", row), P(row, "col"), P(row, "col"), P("col", row)),
        out_specs=(P("col", row), P(row, "col"), P(row, "col"), P("col", row)),
        check_vma=False,
    )
```

```python
import jax
import jax.numpy as jnp
from jax import lax
from jax.experimental import pallas as pl
from jax.experimental.pallas import tpu as pltpu
from jax.sharding import Mesh, PartitionSpec as P

BF16, F32 = jnp.bfloat16, jnp.float32
XY = ("x", "y")
FAR = 4
OFFSETS = (0, 1, -1, 2)
VMEM = pl.BlockSpec(memory_space=pltpu.VMEM)
SMEM = pl.BlockSpec(memory_space=pltpu.SMEM)


def nonlinear(gate, up, hidden_grad):
    sig = jax.nn.sigmoid(gate)
    silu = gate * sig
    hidden = (silu * up).astype(BF16)
    gate_delta = (hidden_grad * up * sig * (1.0 + gate * (1.0 - sig))).astype(BF16)
    up_delta = (hidden_grad * silu).astype(BF16)
    return (hidden, gate_delta, up_delta)


def contract(left, right, left_dim, right_dim):
    return lax.dot_general(
        left, right, (((left_dim,), (right_dim,)), ((), ())), preferred_element_type=F32
    )


def call(body, outs, flops, *args):
    moved = sum(a.size * a.dtype.itemsize for a in (*args, *jax.tree.leaves(outs)))
    return pl.pallas_call(
        body,
        out_shape=outs,
        in_specs=[SMEM if a.dtype == jnp.int32 else VMEM for a in args],
        out_specs=jax.tree.map(lambda _: VMEM, outs),
        compiler_params=pltpu.CompilerParams(vmem_limit_bytes=32 * 2**20),
        cost_estimate=pl.CostEstimate(flops=flops, bytes_accessed=moved, transcendentals=0),
    )(*args)


def half_rows(which, kind, near, second_low, second_high):
    rows = []
    for far in range(2):
        rows += [ref[2 * which + far, kind] for ref in near]
        rows.append(jnp.where(which == 0, second_low[far, kind], second_high[far, kind]))
    return jnp.concatenate(rows, 0)


def send_body(where, a, b, c, d, e, pair, down, pair_out, down_out):
    for kind, weight, out in ((0, pair, pair_out), (1, down, down_out)):
        rows = half_rows(1 - where[0], kind, (a, b, c), d, e)
        out[...] = contract(rows, weight[...], 1, 1).reshape(out.shape)


def keep_body(where, a, b, c, d, e, pair, down, got_pair, got_down, out):
    blocks, rows, _ = out.shape
    wide = pair.shape[0]
    for kind, weight, got, lanes in (
        (0, pair, got_pair, slice(0, wide)),
        (1, down, got_down, slice(wide, None)),
    ):
        mine = half_rows(where[0], kind, (a, b, c), d, e)
        total = contract(mine, weight[...], 1, 1).reshape(blocks, rows, -1)
        out[:, :, lanes] = (total + got[...]).astype(BF16)


def middle_body(parts, deltas, hidden):
    units = parts.shape[2] // 3
    total = parts[0].astype(F32)
    for i in range(1, parts.shape[0]):
        total += parts[i].astype(F32)
    hid, gate_delta, up_delta = nonlinear(
        total[:, :units], total[:, units : 2 * units], total[:, 2 * units :]
    )
    hidden[:, :units] = hid.astype(hidden.dtype)
    if parts.shape[2] // 3 > units:
        hidden[:, units:] = jnp.zeros_like(hidden[:, units:])
    row = jnp.concatenate([gate_delta, up_delta], 1)
    deltas[...] = jnp.broadcast_to(row[None], deltas.shape)


def part_of(deltas, pair):
    lanes = pair.shape[0]
    rows = deltas[...].reshape(-1, deltas.shape[-1])[:, :lanes]
    return contract(rows, pair[...], 1, 0).astype(BF16)


def own_body(deltas, pair, out):
    out[...] = part_of(deltas, pair)


def other_body(where, deltas, pair, own, out):
    devices, tokens, _ = out.shape
    parts = (own[...], part_of(deltas, pair))
    for far in range(2):
        for k, offset in enumerate(OFFSETS):
            start = (far * len(OFFSETS) + k) * tokens
            for half, part in zip((where[0], 1 - where[0]), parts, strict=True):
                device = lax.rem(where[1] + devices + offset + FAR * (2 * half + far), devices)
                out[device] = part[start : start + tokens]


def grads_body(where, a, b, c, d, e, own, other, gate_out, up_out):
    units = gate_out.shape[0]
    deltas = [ref[...].reshape(-1, ref.shape[-1]) for ref in (own, other)]

    def total_of(kind, lanes):
        halves = (where[0], 1 - where[0])
        rows = jnp.concatenate([half_rows(h, kind, (a, b, c), d, e) for h in halves], 0)
        return contract(jnp.concatenate([m[:, lanes] for m in deltas], 0), rows, 0, 0).astype(BF16)

    pair = total_of(0, slice(0, 2 * units))
    gate_out[...] = pair[:units]
    up_out[...] = pair[units:]


def down_body(where, a, b, c, d, e, hidden, out):
    units = out.shape[0]
    total = jnp.zeros(out.shape, F32)
    for half in range(2):
        rows = half_rows(half, 1, (a, b, c), d, e)
        left = hidden[:, half, :, :units].astype(BF16).reshape(rows.shape[0], units)
        total += contract(left, rows, 0, 0)
    out[...] = total.astype(BF16)


def swap_cores(value):
    return lax.ppermute(value, "core", [(0, 1), (1, 0)])


def shift(value, by):
    return lax.ppermute(value, "col", [((i + by) % 16, i) for i in range(16)])


def per_device(inputs, out_grad, gate_weight, up_weight, down_weight):
    tokens, width = inputs.shape
    units = gate_weight.shape[1]
    n = 16
    half = n * tokens // 2
    core, col = lax.axis_index("core"), lax.axis_index("col")
    where = jnp.stack([core, col]).astype(jnp.int32)
    pair = jnp.concatenate([gate_weight.T, up_weight.T], 0)

    both = jnp.stack([inputs, out_grad])
    group = jnp.stack([both, shift(both, FAR), shift(both, 2 * FAR), shift(both, -FAR)])
    after, before = shift(group, 1), shift(group, -1)
    low = shift(group[:2], 2)
    high = shift(jnp.concatenate([group[3:], group[:1]]), -2)
    held = (group, after, before, low, high)

    flops = 2 * half * units * width
    sds = jax.ShapeDtypeStruct
    sent = call(
        send_body,
        (sds((n, half // n, 2 * units), F32), sds((n, half // n, units), F32)),
        3 * flops,
        where,
        *held,
        pair,
        down_weight,
    )
    sent = [swap_cores(value) for value in sent]
    parts = call(
        keep_body, sds((n, half // n, 3 * units), BF16), 3 * flops, where, *held, pair, down_weight, *sent
    )
    parts = lax.all_to_all(parts, XY, 0, 0)
    row, hidden = call(
        middle_body,
        (sds((n, half // n, 2 * units), BF16), sds((half // n, 1024), F32)),
        40 * half // n * units,
        parts,
    )
    hidden = lax.all_gather(hidden, ("x", "y", "core"), axis=0)
    own = lax.all_to_all(row, XY, 0, 0)
    other = swap_cores(own)
    own_part = call(own_body, sds((half, width), BF16), 2 * flops, own, pair)
    pieces = call(
        other_body, sds((n, tokens, width), BF16), 2 * flops, where, other, pair, own_part
    )
    pieces = lax.all_to_all(pieces, "col", 0, 0)
    grad = sds((units, width), BF16)
    input_grad = jnp.sum(pieces.astype(F32), axis=0).astype(BF16)
    gate_grad, up_grad = call(
        grads_body,
        (grad, grad),
        6 * flops,
        where,
        *held,
        own,
        other,
    )
    hidden = hidden.reshape(n, 2, half // n, -1)
    down_grad = call(down_body, grad, 2 * flops, where, *held, hidden)
    return (input_grad, gate_grad.T, up_grad.T, down_grad)


def solution(mesh):
    grid = Mesh(mesh.devices.reshape(4, 4, 2, 16), ("x", "y", "core", "col"))
    row = ("x", "y", "core")
    return jax.shard_map(
        per_device,
        mesh=grid,
        in_specs=(P("col", row), P("col", row), P(row, "col"), P(row, "col"), P("col", row)),
        out_specs=(P("col", row), P(row, "col"), P(row, "col"), P("col", row)),
        check_vma=False,
    )
```

```python
import jax
import jax.numpy as jnp
from jax import lax
from jax.experimental import pallas as pl
from jax.experimental.pallas import tpu as pltpu
from jax.sharding import Mesh, PartitionSpec as P

BF16, F32 = jnp.bfloat16, jnp.float32
XY = ("x", "y")
FAR = 4
OFFSETS = (0, 1, -1, 2)
VMEM = pl.BlockSpec(memory_space=pltpu.VMEM)
ANY = pl.BlockSpec(memory_space=pl.ANY)
SMEM = pl.BlockSpec(memory_space=pltpu.SMEM)


def nonlinear(gate, up, hidden_grad):
    sig = jax.nn.sigmoid(gate)
    silu = gate * sig
    hidden = (silu * up).astype(BF16)
    gate_delta = (hidden_grad * up * sig * (1.0 + gate * (1.0 - sig))).astype(BF16)
    up_delta = (hidden_grad * silu).astype(BF16)
    return (hidden, gate_delta, up_delta)


def contract(left, right, left_dim, right_dim):
    return lax.dot_general(
        left, right, (((left_dim,), (right_dim,)), ((), ())), preferred_element_type=F32
    )


def call(body, outs, flops, *args, after=()):
    moved = sum(a.size * a.dtype.itemsize for a in (*args, *jax.tree.leaves(outs)))
    return pl.pallas_call(
        body,
        out_shape=outs,
        in_specs=[SMEM if a.dtype == jnp.int32 else VMEM for a in args] + [ANY] * len(after),
        out_specs=jax.tree.map(lambda _: VMEM, outs),
        compiler_params=pltpu.CompilerParams(vmem_limit_bytes=32 * 2**20),
        cost_estimate=pl.CostEstimate(flops=flops, bytes_accessed=moved, transcendentals=0),
    )(*args, *after)


def half_rows(which, kind, near, second_low, second_high):
    rows = []
    for far in range(2):
        rows += [ref[2 * which + far, kind] for ref in near]
        rows.append(jnp.where(which == 0, second_low[far, kind], second_high[far, kind]))
    return jnp.concatenate(rows, 0)


def send_body(where, a, b, c, d, e, pair, down, pair_out, down_out):
    for kind, weight, out in ((0, pair, pair_out), (1, down, down_out)):
        rows = half_rows(1 - where[0], kind, (a, b, c), d, e)
        out[...] = contract(rows, weight[...], 1, 1).reshape(out.shape)


def keep_body(where, a, b, c, d, e, pair, down, got_pair, got_down, out):
    blocks, rows, _ = out.shape
    wide = pair.shape[0]
    for kind, weight, got, lanes in (
        (0, pair, got_pair, slice(0, wide)),
        (1, down, got_down, slice(wide, None)),
    ):
        mine = half_rows(where[0], kind, (a, b, c), d, e)
        total = contract(mine, weight[...], 1, 1).reshape(blocks, rows, -1)
        out[:, :, lanes] = (total + got[...]).astype(BF16)


def middle_body(parts, out):
    units = parts.shape[2] // 3
    total = parts[0].astype(F32)
    for i in range(1, parts.shape[0]):
        total += parts[i].astype(F32)
    hid, gate_delta, up_delta = nonlinear(
        total[:, :units], total[:, units : 2 * units], total[:, 2 * units :]
    )
    row = jnp.concatenate([gate_delta, up_delta, hid], 1)
    out[...] = jnp.broadcast_to(row[None], out.shape)


def part_of(deltas, pair):
    lanes = pair.shape[0]
    rows = deltas[...].reshape(-1, deltas.shape[-1])[:, :lanes]
    return contract(rows, pair[...], 1, 0)


def own_body(deltas, pair, out):
    out[...] = part_of(deltas, pair)


def other_body(where, deltas, pair, own, keep, send):
    slots, tokens, _ = keep.shape
    parts = (own[...], part_of(deltas, pair))
    for far in range(2):
        for k, offset in enumerate(OFFSETS):
            start = (far * len(OFFSETS) + k) * tokens
            for half, part in zip((where[0], 1 - where[0]), parts, strict=True):
                device = where[1] + 2 * slots + offset + FAR * (2 * half + far)
                slot = lax.div(lax.rem(device, 2 * slots), 2)
                rows = part[start : start + tokens]
                if offset % 2:
                    send[slot] = rows.astype(BF16)
                else:
                    keep[slot] = rows


def add_body(keep, got, _, out):
    out[...] = (keep[...] + got[...].astype(F32)).astype(BF16)


def grads_body(where, a, b, c, d, e, own, other, gate_out, up_out, down_out):
    units = gate_out.shape[0]
    deltas = [ref[...].reshape(-1, ref.shape[-1]) for ref in (own, other)]

    def total_of(kind, lanes):
        halves = (where[0], 1 - where[0])
        rows = jnp.concatenate([half_rows(h, kind, (a, b, c), d, e) for h in halves], 0)
        return contract(jnp.concatenate([m[:, lanes] for m in deltas], 0), rows, 0, 0).astype(BF16)

    pair = total_of(0, slice(0, 2 * units))
    gate_out[...] = pair[:units]
    up_out[...] = pair[units:]
    down_out[...] = total_of(1, slice(2 * units, 3 * units))


def swap_cores(value):
    return lax.ppermute(value, "core", [(0, 1), (1, 0)])


def shift(value, by):
    return lax.ppermute(value, "col", [((i + by) % 16, i) for i in range(16)])


def per_device(inputs, out_grad, gate_weight, up_weight, down_weight):
    tokens, width = inputs.shape
    units = gate_weight.shape[1]
    n = 16
    half = n * tokens // 2
    core, col = lax.axis_index("core"), lax.axis_index("col")
    where = jnp.stack([core, col]).astype(jnp.int32)
    pair = jnp.concatenate([gate_weight.T, up_weight.T], 0)

    both = jnp.stack([inputs, out_grad])
    group = jnp.stack([both, shift(both, FAR), shift(both, 2 * FAR), shift(both, -FAR)])
    after, before = shift(group, 1), shift(group, -1)
    low = shift(group[:2], 2)
    high = shift(jnp.concatenate([group[3:], group[:1]]), -2)
    held = (group, after, before, low, high)

    flops = 2 * half * units * width
    sds = jax.ShapeDtypeStruct
    sent = call(
        send_body,
        (sds((n, half // n, 2 * units), F32), sds((n, half // n, units), F32)),
        3 * flops,
        where,
        *held,
        pair,
        down_weight,
    )
    sent = [swap_cores(value) for value in sent]
    parts = call(
        keep_body, sds((n, half // n, 3 * units), BF16), 3 * flops, where, *held, pair, down_weight, *sent
    )
    parts = lax.all_to_all(parts, XY, 0, 0)
    row = call(middle_body, sds(parts.shape, BF16), 40 * half // n * units, parts)
    own = lax.all_to_all(row, XY, 0, 0)
    other = swap_cores(own)
    own_part = call(own_body, sds((half, width), F32), 2 * flops, own, pair)
    slots = (n // 2, tokens, width)
    keep, send = call(
        other_body, (sds(slots, F32), sds(slots, BF16)), 2 * flops, where, other, pair, own_part
    )
    got = lax.ppermute(send, "col", [(i, i ^ 1) for i in range(n)])
    grad = sds((units, width), BF16)
    gate_grad, up_grad, down_grad = call(
        grads_body,
        (grad, grad, grad),
        6 * flops,
        where,
        *held,
        own,
        other,
    )
    pieces = call(add_body, sds(slots, BF16), 0, keep, got, after=(down_grad,))
    parity = [list(range(i, n, 2)) for i in range(2)]
    pieces = lax.all_to_all(pieces, "col", 0, 0, axis_index_groups=parity)
    input_grad = jnp.sum(pieces.astype(F32), axis=0).astype(BF16)
    return (input_grad, gate_grad.T, up_grad.T, down_grad)


def solution(mesh):
    grid = Mesh(mesh.devices.reshape(4, 4, 2, 16), ("x", "y", "core", "col"))
    row = ("x", "y", "core")
    return jax.shard_map(
        per_device,
        mesh=grid,
        in_specs=(P("col", row), P("col", row), P(row, "col"), P(row, "col"), P("col", row)),
        out_specs=(P("col", row), P(row, "col"), P(row, "col"), P("col", row)),
        check_vma=False,
    )
```

```python
import jax
import jax.numpy as jnp
from jax import lax
from jax.experimental import pallas as pl
from jax.experimental.pallas import tpu as pltpu
from jax.sharding import Mesh, PartitionSpec as P

BF16, F32 = jnp.bfloat16, jnp.float32
XY = ("x", "y")
VMEM = pl.BlockSpec(memory_space=pltpu.VMEM)
ANY = pl.BlockSpec(memory_space=pl.ANY)
SMEM = pl.BlockSpec(memory_space=pltpu.SMEM)


def nonlinear(gate, up, hidden_grad):
    sig = jax.nn.sigmoid(gate)
    silu = gate * sig
    hidden = (silu * up).astype(BF16)
    gate_delta = (hidden_grad * up * sig * (1.0 + gate * (1.0 - sig))).astype(BF16)
    up_delta = (hidden_grad * silu).astype(BF16)
    return (hidden, gate_delta, up_delta)


def contract(left, right, left_dim, right_dim):
    return lax.dot_general(
        left, right, (((left_dim,), (right_dim,)), ((), ())), preferred_element_type=F32
    )


def call(body, outs, flops, *args, after=()):
    moved = sum(a.size * a.dtype.itemsize for a in (*args, *jax.tree.leaves(outs)))
    return pl.pallas_call(
        body,
        out_shape=outs,
        in_specs=[SMEM if a.dtype == jnp.int32 else VMEM for a in args] + [ANY] * len(after),
        out_specs=jax.tree.map(lambda _: VMEM, outs),
        compiler_params=pltpu.CompilerParams(vmem_limit_bytes=32 * 2**20),
        cost_estimate=pl.CostEstimate(flops=flops, bytes_accessed=moved, transcendentals=0),
    )(*args, *after)


def half_rows(which, kind, even, low, high):
    count, tokens, width = low.shape[0], *low.shape[2:]
    first = even[pl.ds(which * count, count), kind]
    second = jnp.where(which == 0, low[:, kind], high[:, kind])
    return jnp.concatenate([first, second], 0).reshape(2 * count * tokens, width)


def send_body(where, a, b, c, pair, down, pair_out, down_out):
    for kind, weight, out in ((0, pair, pair_out), (1, down, down_out)):
        rows = half_rows(1 - where[0], kind, a, b, c)
        out[...] = contract(rows, weight[...], 1, 1).reshape(out.shape)


def keep_body(where, a, b, c, pair, down, got_pair, got_down, out):
    blocks, rows, _ = out.shape
    wide = pair.shape[0]
    for kind, weight, got, lanes in (
        (0, pair, got_pair, slice(0, wide)),
        (1, down, got_down, slice(wide, None)),
    ):
        mine = half_rows(where[0], kind, a, b, c)
        total = contract(mine, weight[...], 1, 1).reshape(blocks, rows, -1)
        out[:, :, lanes] = (total + got[...]).astype(BF16)


def middle_body(parts, out):
    units = parts.shape[2] // 3
    total = parts[0].astype(F32)
    for i in range(1, parts.shape[0]):
        total += parts[i].astype(F32)
    hid, gate_delta, up_delta = nonlinear(
        total[:, :units], total[:, units : 2 * units], total[:, 2 * units :]
    )
    row = jnp.concatenate([gate_delta, up_delta, hid], 1)
    out[...] = jnp.broadcast_to(row[None], out.shape)


def part_of(deltas, pair):
    lanes = pair.shape[0]
    rows = deltas[...].reshape(-1, deltas.shape[-1])[:, :lanes]
    return contract(rows, pair[...], 1, 0)


def own_body(deltas, pair, out):
    out[...] = part_of(deltas, pair)


def other_body(where, deltas, pair, own, keep, send):
    count, tokens = keep.shape[0] // 2, keep.shape[1]
    parts = (own[...], part_of(deltas, pair))
    for half, part in zip((where[0], 1 - where[0]), parts, strict=True):
        rows = part.reshape(2 * count, tokens, -1)
        keep[pl.ds(half * count, count)] = rows[:count]
        send[pl.ds(half * count, count)] = rows[count:].astype(BF16)


def add_body(keep, got, _, out):
    out[...] = (keep[...] + got[...].astype(F32)).astype(BF16)


def grads_body(where, a, b, c, own, other, gate_out, up_out, down_out, done):
    done[...] = jnp.zeros_like(done)
    units = gate_out.shape[0]
    deltas = [ref[...].reshape(-1, ref.shape[-1]) for ref in (own, other)]

    def total_of(kind, lanes):
        halves = (where[0], 1 - where[0])
        rows = jnp.concatenate([half_rows(h, kind, a, b, c) for h in halves], 0)
        return contract(jnp.concatenate([m[:, lanes] for m in deltas], 0), rows, 0, 0).astype(BF16)

    pair = total_of(0, slice(0, 2 * units))
    gate_out[...] = pair[:units]
    up_out[...] = pair[units:]
    down_out[...] = total_of(1, slice(2 * units, 3 * units))


def swap_cores(value):
    return lax.ppermute(value, "core", [(0, 1), (1, 0)])


def shift(value, by):
    return lax.ppermute(value, "col", [((i + by) % 16, i) for i in range(16)])


def per_device(inputs, out_grad, gate_weight, up_weight, down_weight):
    tokens, width = inputs.shape
    units = gate_weight.shape[1]
    n = 16
    half = n * tokens // 2
    where = lax.axis_index("core").astype(jnp.int32).reshape(1)
    pair = jnp.concatenate([gate_weight.T, up_weight.T], 0)

    parity = [list(range(i, n, 2)) for i in range(2)]
    both = jnp.stack([inputs, out_grad])
    even = lax.all_gather(both, "col", axis=0, axis_index_groups=parity)
    low, high = shift(even[: n // 4], 1), shift(even[n // 4 :], -1)
    held = (even, low, high)

    flops = 2 * half * units * width
    sds = jax.ShapeDtypeStruct
    sent = call(
        send_body,
        (sds((n, half // n, 2 * units), F32), sds((n, half // n, units), F32)),
        3 * flops,
        where,
        *held,
        pair,
        down_weight,
    )
    sent = [swap_cores(value) for value in sent]
    parts = call(
        keep_body, sds((n, half // n, 3 * units), BF16), 3 * flops, where, *held, pair, down_weight, *sent
    )
    parts = lax.all_to_all(parts, XY, 0, 0)
    row = call(middle_body, sds(parts.shape, BF16), 40 * half // n * units, parts)
    own = lax.all_to_all(row, XY, 0, 0)
    other = swap_cores(own)
    own_part = call(own_body, sds((half, width), F32), 2 * flops, own, pair)
    slots = (n // 2, tokens, width)
    keep, send = call(
        other_body, (sds(slots, F32), sds(slots, BF16)), 2 * flops, where, other, pair, own_part
    )
    got = lax.ppermute(send, "col", [(i, i ^ 1) for i in range(n)])
    grad = sds((units, width), BF16)
    gate_grad, up_grad, down_grad, done = call(
        grads_body,
        (grad, grad, grad, sds((8, 128), F32)),
        6 * flops,
        where,
        *held,
        own,
        other,
    )
    pieces = call(add_body, sds(slots, BF16), 0, keep, got, after=(done,))
    pieces = lax.all_to_all(pieces, "col", 0, 0, axis_index_groups=parity)
    input_grad = jnp.sum(pieces.astype(F32), axis=0).astype(BF16)
    return (input_grad, gate_grad.T, up_grad.T, down_grad)


def solution(mesh):
    grid = Mesh(mesh.devices.reshape(4, 4, 2, 16), ("x", "y", "core", "col"))
    row = ("x", "y", "core")
    return jax.shard_map(
        per_device,
        mesh=grid,
        in_specs=(P("col", row), P("col", row), P(row, "col"), P(row, "col"), P("col", row)),
        out_specs=(P("col", row), P(row, "col"), P(row, "col"), P("col", row)),
        check_vma=False,
    )
```

```python
import jax
import jax.numpy as jnp
from jax import lax
from jax.experimental import pallas as pl
from jax.experimental.pallas import tpu as pltpu
from jax.sharding import Mesh, PartitionSpec as P

BF16, F32 = jnp.bfloat16, jnp.float32
XY = ("x", "y")
VMEM = pl.BlockSpec(memory_space=pltpu.VMEM)
ANY = pl.BlockSpec(memory_space=pl.ANY)
SMEM = pl.BlockSpec(memory_space=pltpu.SMEM)


def nonlinear(gate, up, hidden_grad):
    sig = jax.nn.sigmoid(gate)
    silu = gate * sig
    hidden = (silu * up).astype(BF16)
    gate_delta = (hidden_grad * up * sig * (1.0 + gate * (1.0 - sig))).astype(BF16)
    up_delta = (hidden_grad * silu).astype(BF16)
    return (hidden, gate_delta, up_delta)


def contract(left, right, left_dim, right_dim):
    return lax.dot_general(
        left, right, (((left_dim,), (right_dim,)), ((), ())), preferred_element_type=F32
    )


def call(body, outs, flops, *args, after=()):
    moved = sum(a.size * a.dtype.itemsize for a in (*args, *jax.tree.leaves(outs)))
    return pl.pallas_call(
        body,
        out_shape=outs,
        in_specs=[SMEM if a.dtype == jnp.int32 else VMEM for a in args] + [ANY] * len(after),
        out_specs=jax.tree.map(lambda _: VMEM, outs),
        compiler_params=pltpu.CompilerParams(vmem_limit_bytes=32 * 2**20),
        cost_estimate=pl.CostEstimate(flops=flops, bytes_accessed=moved, transcendentals=0),
    )(*args, *after)


def flat(value):
    return value.reshape(-1, value.shape[-1])


def first_rows(which, kind, even):
    count = even.shape[0] // 2
    return flat(even[pl.ds(which * count, count), kind])


def second_rows(which, kind, low, high):
    return flat(jnp.where(which == 0, low[:, kind], high[:, kind]))


def send_body(rows, weights, out):
    end = 0
    for kind, weight in enumerate(weights):
        lanes = slice(end, end + weight.shape[0])
        end = lanes.stop
        part = contract(rows(kind), weight[...], 1, 1)
        out[:, :, lanes] = part.reshape(*out.shape[:2], -1)


def send_first_body(where, even, pair, down, out):
    send_body(lambda kind: first_rows(1 - where[0], kind, even), (pair, down), out)


def send_second_body(where, low, high, pair, down, out):
    send_body(lambda kind: second_rows(1 - where[0], kind, low, high), (pair, down), out)


def half_rows(which, kind, even, low, high):
    return jnp.concatenate(
        [first_rows(which, kind, even), second_rows(which, kind, low, high)], 0
    )


def keep_body(where, even, low, high, pair, down, got_first, got_second, out):
    blocks, rows, _ = out.shape
    wide, mid = pair.shape[0], blocks // 2
    for kind, weight, lanes in ((0, pair, slice(0, wide)), (1, down, slice(wide, None))):
        mine = half_rows(where[0], kind, even, low, high)
        total = contract(mine, weight[...], 1, 1).reshape(blocks, rows, -1)
        out[:mid, :, lanes] = (total[:mid] + got_first[:, :, lanes]).astype(BF16)
        out[mid:, :, lanes] = (total[mid:] + got_second[:, :, lanes]).astype(BF16)


def middle_body(parts, out):
    units = parts.shape[2] // 3
    total = parts[0].astype(F32)
    for i in range(1, parts.shape[0]):
        total += parts[i].astype(F32)
    hid, gate_delta, up_delta = nonlinear(
        total[:, :units], total[:, units : 2 * units], total[:, 2 * units :]
    )
    row = jnp.concatenate([gate_delta, up_delta, hid], 1)
    out[...] = jnp.broadcast_to(row[None], out.shape)


def part_of(deltas, pair):
    lanes = pair.shape[0]
    rows = deltas[...].reshape(-1, deltas.shape[-1])[:, :lanes]
    return contract(rows, pair[...], 1, 0)


def own_body(deltas, pair, out):
    out[...] = part_of(deltas, pair)


def other_body(where, deltas, pair, own, keep, send_low, send_high):
    count, tokens = keep.shape[0] // 2, keep.shape[1]
    mine = own[...].reshape(2 * count, tokens, -1)
    other = part_of(deltas, pair).reshape(2 * count, tokens, -1)
    keep[pl.ds(where[0] * count, count)] = mine[:count]
    keep[pl.ds((1 - where[0]) * count, count)] = other[:count]
    mine, other = mine[count:].astype(BF16), other[count:].astype(BF16)
    send_low[...] = jnp.where(where[0] == 0, mine, other)
    send_high[...] = jnp.where(where[0] == 0, other, mine)


def add_body(keep, got_low, got_high, _, out):
    count = keep.shape[0] // 2
    out[:count] = (keep[:count] + got_low[...].astype(F32)).astype(BF16)
    out[count:] = (keep[count:] + got_high[...].astype(F32)).astype(BF16)


def grads_body(where, a, b, c, own, other, gate_out, up_out, down_out, done):
    done[...] = jnp.zeros_like(done)
    units = gate_out.shape[0]
    deltas = [ref[...].reshape(-1, ref.shape[-1]) for ref in (own, other)]

    def total_of(kind, lanes):
        halves = (where[0], 1 - where[0])
        rows = jnp.concatenate([half_rows(h, kind, a, b, c) for h in halves], 0)
        return contract(jnp.concatenate([m[:, lanes] for m in deltas], 0), rows, 0, 0).astype(BF16)

    pair = total_of(0, slice(0, 2 * units))
    gate_out[...] = pair[:units]
    up_out[...] = pair[units:]
    down_out[...] = total_of(1, slice(2 * units, 3 * units))


def swap_cores(value):
    return lax.ppermute(value, "core", [(0, 1), (1, 0)])


def shift(value, by):
    return lax.ppermute(value, "col", [((i + by) % 16, i) for i in range(16)])


def per_device(inputs, out_grad, gate_weight, up_weight, down_weight):
    tokens, width = inputs.shape
    units = gate_weight.shape[1]
    n = 16
    half = n * tokens // 2
    where = lax.axis_index("core").astype(jnp.int32).reshape(1)
    pair = jnp.concatenate([gate_weight.T, up_weight.T], 0)

    parity = [list(range(i, n, 2)) for i in range(2)]
    both = jnp.stack([inputs, out_grad])
    even = lax.all_gather(both, "col", axis=0, axis_index_groups=parity)
    low, high = shift(even[: n // 4], 1), shift(even[n // 4 :], -1)
    held = (even, low, high)

    flops = 2 * half * units * width
    sds = jax.ShapeDtypeStruct
    sent = sds((n // 2, half // n, 3 * units), F32)
    weights = (pair, down_weight)
    first = swap_cores(call(send_first_body, sent, 3 * flops // 2, where, even, *weights))
    second = swap_cores(call(send_second_body, sent, 3 * flops // 2, where, low, high, *weights))
    parts = call(
        keep_body,
        sds((n, half // n, 3 * units), BF16),
        3 * flops,
        where,
        *held,
        *weights,
        first,
        second,
    )
    parts = lax.all_to_all(parts, XY, 0, 0)
    row = call(middle_body, sds(parts.shape, BF16), 40 * half // n * units, parts)
    own = lax.all_to_all(row, XY, 0, 0)
    other = swap_cores(own)
    own_part = call(own_body, sds((half, width), F32), 2 * flops, own, pair)
    slots, some = (n // 2, tokens, width), sds((n // 4, tokens, width), BF16)
    keep, send_low, send_high = call(
        other_body, (sds(slots, F32), some, some), 2 * flops, where, other, pair, own_part
    )
    got = (shift(send_low, 1), shift(send_high, -1))
    grad = sds((units, width), BF16)
    gate_grad, up_grad, down_grad, done = call(
        grads_body,
        (grad, grad, grad, sds((8, 128), F32)),
        6 * flops,
        where,
        *held,
        own,
        other,
    )
    pieces = call(add_body, sds(slots, BF16), 0, keep, *got, after=(done,))
    pieces = lax.all_to_all(pieces, "col", 0, 0, axis_index_groups=parity)
    input_grad = jnp.sum(pieces.astype(F32), axis=0).astype(BF16)
    return (input_grad, gate_grad.T, up_grad.T, down_grad)


def solution(mesh):
    grid = Mesh(mesh.devices.reshape(4, 4, 2, 16), ("x", "y", "core", "col"))
    row = ("x", "y", "core")
    return jax.shard_map(
        per_device,
        mesh=grid,
        in_specs=(P("col", row), P("col", row), P(row, "col"), P(row, "col"), P("col", row)),
        out_specs=(P("col", row), P(row, "col"), P(row, "col"), P("col", row)),
        check_vma=False,
    )
```

```python
import jax
import jax.numpy as jnp
from jax import lax
from jax.experimental import pallas as pl
from jax.experimental.pallas import tpu as pltpu
from jax.sharding import Mesh, PartitionSpec as P

BF16, F32 = jnp.bfloat16, jnp.float32
XY = ("x", "y")
VMEM = pl.BlockSpec(memory_space=pltpu.VMEM)
ANY = pl.BlockSpec(memory_space=pl.ANY)
SMEM = pl.BlockSpec(memory_space=pltpu.SMEM)


def nonlinear(gate, up, hidden_grad):
    sig = jax.nn.sigmoid(gate)
    silu = gate * sig
    hidden = (silu * up).astype(BF16)
    gate_delta = (hidden_grad * up * sig * (1.0 + gate * (1.0 - sig))).astype(BF16)
    up_delta = (hidden_grad * silu).astype(BF16)
    return (hidden, gate_delta, up_delta)


def contract(left, right, left_dim, right_dim):
    return lax.dot_general(
        left, right, (((left_dim,), (right_dim,)), ((), ())), preferred_element_type=F32
    )


def call(body, outs, flops, *args, after=()):
    moved = sum(a.size * a.dtype.itemsize for a in (*args, *jax.tree.leaves(outs)))
    return pl.pallas_call(
        body,
        out_shape=outs,
        in_specs=[SMEM if a.dtype == jnp.int32 else VMEM for a in args] + [ANY] * len(after),
        out_specs=jax.tree.map(lambda _: VMEM, outs),
        compiler_params=pltpu.CompilerParams(vmem_limit_bytes=32 * 2**20),
        cost_estimate=pl.CostEstimate(flops=flops, bytes_accessed=moved, transcendentals=0),
    )(*args, *after)


def flat(value):
    return value.reshape(-1, value.shape[-1])


def first_rows(which, kind, even):
    count = even.shape[0] // 2
    return flat(even[pl.ds(which * count, count), kind])


def second_rows(which, kind, low, high):
    return flat(jnp.where(which == 0, low[:, kind], high[:, kind]))


def send_body(rows, weights, out):
    end = 0
    for kind, weight in enumerate(weights):
        lanes = slice(end, end + weight.shape[0])
        end = lanes.stop
        part = contract(rows(kind), weight[...], 1, 1)
        out[:, :, lanes] = part.reshape(*out.shape[:2], -1)


def send_first_body(where, even, pair, down, out):
    send_body(lambda kind: first_rows(1 - where[0], kind, even), (pair, down), out)


def send_second_body(where, low, high, pair, down, out):
    send_body(lambda kind: second_rows(1 - where[0], kind, low, high), (pair, down), out)


def half_rows(which, kind, even, low, high):
    return jnp.concatenate(
        [first_rows(which, kind, even), second_rows(which, kind, low, high)], 0
    )


def keep_body(where, even, low, high, pair, down, got_first, got_second, out):
    blocks, rows, _ = out.shape
    wide, mid = pair.shape[0], blocks // 2
    for kind, weight, lanes in ((0, pair, slice(0, wide)), (1, down, slice(wide, None))):
        mine = half_rows(where[0], kind, even, low, high)
        total = contract(mine, weight[...], 1, 1).reshape(blocks, rows, -1)
        out[:mid, :, lanes] = (total[:mid] + got_first[:, :, lanes]).astype(BF16)
        out[mid:, :, lanes] = (total[mid:] + got_second[:, :, lanes]).astype(BF16)


def middle_body(parts, out):
    units = parts.shape[2] // 3
    total = parts[0].astype(F32)
    for i in range(1, parts.shape[0]):
        total += parts[i].astype(F32)
    hid, gate_delta, up_delta = nonlinear(
        total[:, :units], total[:, units : 2 * units], total[:, 2 * units :]
    )
    row = jnp.concatenate([gate_delta, up_delta, hid], 1)
    out[...] = jnp.broadcast_to(row[None], out.shape)


def part_of(deltas, pair):
    lanes = pair.shape[0]
    rows = deltas[...].reshape(-1, deltas.shape[-1])[:, :lanes]
    return contract(rows, pair[...], 1, 0)


def part_body(deltas, pair, keep, send):
    part = part_of(deltas, pair).reshape(2 * keep.shape[0], *keep.shape[1:])
    keep[...] = part[: keep.shape[0]]
    send[...] = part[keep.shape[0] :].astype(BF16)


def add_body(where, keep_own, got_own, keep_other, got_other, _, out):
    count = keep_own.shape[0]
    for half, keep, got in ((where[0], keep_own, got_own), (1 - where[0], keep_other, got_other)):
        out[pl.ds(half * count, count)] = (keep[...] + got[...].astype(F32)).astype(BF16)


def grads_body(where, a, b, c, own, other, gate_out, up_out, down_out, done):
    done[...] = jnp.zeros_like(done)
    units = gate_out.shape[0]
    deltas = [ref[...].reshape(-1, ref.shape[-1]) for ref in (own, other)]

    def total_of(kind, lanes):
        halves = (where[0], 1 - where[0])
        rows = jnp.concatenate([half_rows(h, kind, a, b, c) for h in halves], 0)
        return contract(jnp.concatenate([m[:, lanes] for m in deltas], 0), rows, 0, 0).astype(BF16)

    pair = total_of(0, slice(0, 2 * units))
    gate_out[...] = pair[:units]
    up_out[...] = pair[units:]
    down_out[...] = total_of(1, slice(2 * units, 3 * units))


def swap_cores(value):
    return lax.ppermute(value, "core", [(0, 1), (1, 0)])


def from_neighbour(value, by):
    pairs = [(c * 16 + (i + by[c]) % 16, c * 16 + i) for c in range(2) for i in range(16)]
    return lax.ppermute(value, ("core", "col"), pairs)


def per_device(inputs, out_grad, gate_weight, up_weight, down_weight):
    tokens, width = inputs.shape
    units = gate_weight.shape[1]
    n = 16
    half = n * tokens // 2
    where = lax.axis_index("core").astype(jnp.int32).reshape(1)
    pair = jnp.concatenate([gate_weight.T, up_weight.T], 0)

    parity = [list(range(i, n, 2)) for i in range(2)]
    both = jnp.stack([inputs, out_grad])
    even = lax.all_gather(both, "col", axis=0, axis_index_groups=parity)
    low = from_neighbour(even[: n // 4], (1, 1))
    high = from_neighbour(even[n // 4 :], (-1, -1))
    held = (even, low, high)

    flops = 2 * half * units * width
    sds = jax.ShapeDtypeStruct
    sent = sds((n // 2, half // n, 3 * units), F32)
    weights = (pair, down_weight)
    first = swap_cores(call(send_first_body, sent, 3 * flops // 2, where, even, *weights))
    second = swap_cores(call(send_second_body, sent, 3 * flops // 2, where, low, high, *weights))
    parts = call(
        keep_body,
        sds((n, half // n, 3 * units), BF16),
        3 * flops,
        where,
        *held,
        *weights,
        first,
        second,
    )
    parts = lax.all_to_all(parts, XY, 0, 0)
    row = call(middle_body, sds(parts.shape, BF16), 40 * half // n * units, parts)
    own = lax.all_to_all(row, XY, 0, 0)
    other = swap_cores(own)
    some = (n // 4, tokens, width)
    outs = (sds(some, F32), sds(some, BF16))
    keep_own, send_own = call(part_body, outs, 2 * flops, own, pair)
    got_own = from_neighbour(send_own, (1, -1))
    keep_other, send_other = call(part_body, outs, 2 * flops, other, pair)
    got_other = from_neighbour(send_other, (-1, 1))
    grad = sds((units, width), BF16)
    gate_grad, up_grad, down_grad, done = call(
        grads_body,
        (grad, grad, grad, sds((8, 128), F32)),
        6 * flops,
        where,
        *held,
        own,
        other,
    )
    added = (keep_own, got_own, keep_other, got_other)
    pieces = call(add_body, sds((n // 2, tokens, width), BF16), 0, where, *added, after=(done,))
    pieces = lax.all_to_all(pieces, "col", 0, 0, axis_index_groups=parity)
    input_grad = jnp.sum(pieces.astype(F32), axis=0).astype(BF16)
    return (input_grad, gate_grad.T, up_grad.T, down_grad)


def solution(mesh):
    grid = Mesh(mesh.devices.reshape(4, 4, 2, 16), ("x", "y", "core", "col"))
    row = ("x", "y", "core")
    return jax.shard_map(
        per_device,
        mesh=grid,
        in_specs=(P("col", row), P("col", row), P(row, "col"), P(row, "col"), P("col", row)),
        out_specs=(P("col", row), P(row, "col"), P(row, "col"), P("col", row)),
        check_vma=False,
    )
```

```python
import jax
import jax.numpy as jnp
from jax import lax
from jax.experimental import pallas as pl
from jax.experimental.pallas import tpu as pltpu
from jax.sharding import Mesh, PartitionSpec as P

BF16, F32 = jnp.bfloat16, jnp.float32
XY = ("x", "y")
VMEM = pl.BlockSpec(memory_space=pltpu.VMEM)
ANY = pl.BlockSpec(memory_space=pl.ANY)
SMEM = pl.BlockSpec(memory_space=pltpu.SMEM)


def nonlinear(gate, up, hidden_grad):
    sig = jax.nn.sigmoid(gate)
    silu = gate * sig
    hidden = (silu * up).astype(BF16)
    gate_delta = (hidden_grad * up * sig * (1.0 + gate * (1.0 - sig))).astype(BF16)
    up_delta = (hidden_grad * silu).astype(BF16)
    return (hidden, gate_delta, up_delta)


def contract(left, right, left_dim, right_dim):
    return lax.dot_general(
        left, right, (((left_dim,), (right_dim,)), ((), ())), preferred_element_type=F32
    )


def call(body, outs, flops, *args, after=()):
    moved = sum(a.size * a.dtype.itemsize for a in (*args, *jax.tree.leaves(outs)))
    return pl.pallas_call(
        body,
        out_shape=outs,
        in_specs=[SMEM if a.dtype == jnp.int32 else VMEM for a in args] + [ANY] * len(after),
        out_specs=jax.tree.map(lambda _: VMEM, outs),
        compiler_params=pltpu.CompilerParams(vmem_limit_bytes=32 * 2**20),
        cost_estimate=pl.CostEstimate(flops=flops, bytes_accessed=moved, transcendentals=0),
    )(*args, *after)


def flat(value):
    return value.reshape(-1, value.shape[-1])


def first_rows(which, kind, even):
    count = even.shape[0] // 2
    return flat(even[pl.ds(which * count, count), kind])


def send_body(rows, weights, out):
    end = 0
    for kind, weight in enumerate(weights):
        lanes = slice(end, end + weight.shape[0])
        end = lanes.stop
        part = contract(rows(kind), weight[...], 1, 1)
        out[:, :, lanes] = part.reshape(*out.shape[:2], -1)


def send_first_body(where, even, pair, down, out):
    send_body(lambda kind: first_rows(1 - where[0], kind, even), (pair, down), out)


def send_second_body(theirs, pair, down, out):
    send_body(lambda kind: flat(theirs[:, kind]), (pair, down), out)


def half_rows(which, kind, even, odd):
    return jnp.concatenate([first_rows(which, kind, even), flat(odd[:, kind])], 0)


def keep_body(where, even, mine, pair, down, got_first, got_second, out):
    blocks, rows, _ = out.shape
    wide, mid = pair.shape[0], blocks // 2
    for kind, weight, lanes in ((0, pair, slice(0, wide)), (1, down, slice(wide, None))):
        rows_in = half_rows(where[0], kind, even, mine)
        total = contract(rows_in, weight[...], 1, 1).reshape(blocks, rows, -1)
        out[:mid, :, lanes] = (total[:mid] + got_first[:, :, lanes]).astype(BF16)
        out[mid:, :, lanes] = (total[mid:] + got_second[:, :, lanes]).astype(BF16)


def middle_body(parts, out):
    units = parts.shape[2] // 3
    total = parts[0].astype(F32)
    for i in range(1, parts.shape[0]):
        total += parts[i].astype(F32)
    hid, gate_delta, up_delta = nonlinear(
        total[:, :units], total[:, units : 2 * units], total[:, 2 * units :]
    )
    row = jnp.concatenate([gate_delta, up_delta, hid], 1)
    out[...] = jnp.broadcast_to(row[None], out.shape)


def part_of(deltas, pair):
    lanes = pair.shape[0]
    rows = deltas[...].reshape(-1, deltas.shape[-1])[:, :lanes]
    return contract(rows, pair[...], 1, 0)


def part_body(deltas, pair, keep, send):
    part = part_of(deltas, pair).reshape(2 * keep.shape[0], *keep.shape[1:])
    keep[...] = part[: keep.shape[0]]
    send[...] = part[keep.shape[0] :].astype(BF16)


def add_body(where, keep_own, got_own, keep_other, got_other, _, out):
    count = keep_own.shape[0]
    for half, keep, got in ((where[0], keep_own, got_own), (1 - where[0], keep_other, got_other)):
        out[pl.ds(half * count, count)] = (keep[...] + got[...].astype(F32)).astype(BF16)


def grads_body(where, even, mine, theirs, own, other, gate_out, up_out, down_out, done):
    done[...] = jnp.zeros_like(done)
    units = gate_out.shape[0]
    deltas = [ref[...].reshape(-1, ref.shape[-1]) for ref in (own, other)]

    def total_of(kind, lanes):
        halves = ((where[0], mine), (1 - where[0], theirs))
        rows = jnp.concatenate([half_rows(h, kind, even, odd) for h, odd in halves], 0)
        return contract(jnp.concatenate([m[:, lanes] for m in deltas], 0), rows, 0, 0).astype(BF16)

    pair = total_of(0, slice(0, 2 * units))
    gate_out[...] = pair[:units]
    up_out[...] = pair[units:]
    down_out[...] = total_of(1, slice(2 * units, 3 * units))


def swap_cores(value):
    return lax.ppermute(value, "core", [(0, 1), (1, 0)])


def from_neighbour(value, by):
    pairs = [(c * 16 + (i + by[c]) % 16, c * 16 + i) for c in range(2) for i in range(16)]
    return lax.ppermute(value, ("core", "col"), pairs)


def per_device(inputs, out_grad, gate_weight, up_weight, down_weight):
    tokens, width = inputs.shape
    units = gate_weight.shape[1]
    n = 16
    half = n * tokens // 2
    where = lax.axis_index("core").astype(jnp.int32).reshape(1)
    pair = jnp.concatenate([gate_weight.T, up_weight.T], 0)

    parity = [list(range(i, n, 2)) for i in range(2)]
    both = jnp.stack([inputs, out_grad])
    even = lax.all_gather(both, "col", axis=0, axis_index_groups=parity)
    count, core = n // 4, lax.axis_index("core")
    parts_of = [lax.dynamic_slice_in_dim(even, c * count, count, 0) for c in (1 - core, core)]
    theirs, mine = from_neighbour(parts_of[0], (-1, 1)), from_neighbour(parts_of[1], (1, -1))

    flops = 2 * half * units * width
    sds = jax.ShapeDtypeStruct
    sent = sds((n // 2, half // n, 3 * units), F32)
    weights = (pair, down_weight)
    first = swap_cores(call(send_first_body, sent, 3 * flops // 2, where, even, *weights))
    second = swap_cores(call(send_second_body, sent, 3 * flops // 2, theirs, *weights))
    parts = call(
        keep_body,
        sds((n, half // n, 3 * units), BF16),
        3 * flops,
        where,
        even,
        mine,
        *weights,
        first,
        second,
    )
    parts = lax.all_to_all(parts, XY, 0, 0)
    row = call(middle_body, sds(parts.shape, BF16), 40 * half // n * units, parts)
    own = lax.all_to_all(row, XY, 0, 0)
    other = swap_cores(own)
    some = (n // 4, tokens, width)
    outs = (sds(some, F32), sds(some, BF16))
    keep_own, send_own = call(part_body, outs, 2 * flops, own, pair)
    got_own = from_neighbour(send_own, (1, -1))
    keep_other, send_other = call(part_body, outs, 2 * flops, other, pair)
    got_other = from_neighbour(send_other, (-1, 1))
    grad = sds((units, width), BF16)
    gate_grad, up_grad, down_grad, done = call(
        grads_body,
        (grad, grad, grad, sds((8, 128), F32)),
        6 * flops,
        where,
        even,
        mine,
        theirs,
        own,
        other,
    )
    added = (keep_own, got_own, keep_other, got_other)
    pieces = call(add_body, sds((n // 2, tokens, width), BF16), 0, where, *added, after=(done,))
    pieces = lax.all_to_all(pieces, "col", 0, 0, axis_index_groups=parity)
    input_grad = jnp.sum(pieces.astype(F32), axis=0).astype(BF16)
    return (input_grad, gate_grad.T, up_grad.T, down_grad)


def solution(mesh):
    grid = Mesh(mesh.devices.reshape(4, 4, 2, 16), ("x", "y", "core", "col"))
    row = ("x", "y", "core")
    return jax.shard_map(
        per_device,
        mesh=grid,
        in_specs=(P("col", row), P("col", row), P(row, "col"), P(row, "col"), P("col", row)),
        out_specs=(P("col", row), P(row, "col"), P(row, "col"), P("col", row)),
        check_vma=False,
    )
```

```python
import jax
import jax.numpy as jnp
from jax import lax
from jax.experimental import pallas as pl
from jax.experimental.pallas import tpu as pltpu
from jax.sharding import Mesh, PartitionSpec as P

BF16, F32 = jnp.bfloat16, jnp.float32
XY = ("x", "y")
VMEM = pl.BlockSpec(memory_space=pltpu.VMEM)
ANY = pl.BlockSpec(memory_space=pl.ANY)
SMEM = pl.BlockSpec(memory_space=pltpu.SMEM)


def nonlinear(gate, up, hidden_grad):
    sig = jax.nn.sigmoid(gate)
    silu = gate * sig
    hidden = (silu * up).astype(BF16)
    gate_delta = (hidden_grad * up * sig * (1.0 + gate * (1.0 - sig))).astype(BF16)
    up_delta = (hidden_grad * silu).astype(BF16)
    return (hidden, gate_delta, up_delta)


def contract(left, right, left_dim, right_dim):
    return lax.dot_general(
        left, right, (((left_dim,), (right_dim,)), ((), ())), preferred_element_type=F32
    )


def call(body, outs, flops, *args, after=()):
    moved = sum(a.size * a.dtype.itemsize for a in (*args, *jax.tree.leaves(outs)))
    return pl.pallas_call(
        body,
        out_shape=outs,
        in_specs=[SMEM if a.dtype == jnp.int32 else VMEM for a in args] + [ANY] * len(after),
        out_specs=jax.tree.map(lambda _: VMEM, outs),
        compiler_params=pltpu.CompilerParams(vmem_limit_bytes=32 * 2**20),
        cost_estimate=pl.CostEstimate(flops=flops, bytes_accessed=moved, transcendentals=0),
    )(*args, *after)


def flat(value):
    return value.reshape(-1, value.shape[-1])


def first_rows(which, kind, even):
    count = even.shape[0] // 2
    return flat(even[pl.ds(which * count, count), kind])


def send_body(rows, weights, out):
    end = 0
    for kind, weight in enumerate(weights):
        lanes = slice(end, end + weight.shape[0])
        end = lanes.stop
        part = contract(rows(kind), weight[...], 1, 1)
        out[:, :, lanes] = part.reshape(*out.shape[:2], -1)


def send_first_body(where, even, pair, down, out):
    send_body(lambda kind: first_rows(1 - where[0], kind, even), (pair, down), out)


def send_second_body(theirs, pair, down, _, out):
    send_body(lambda kind: flat(theirs[:, kind]), (pair, down), out)


def half_rows(which, kind, even, odd):
    return jnp.concatenate([first_rows(which, kind, even), flat(odd[:, kind])], 0)


def keep_body(where, even, mine, pair, down, got_first, got_second, out):
    blocks, rows, _ = out.shape
    wide, mid = pair.shape[0], blocks // 2
    for kind, weight, lanes in ((0, pair, slice(0, wide)), (1, down, slice(wide, None))):
        rows_in = half_rows(where[0], kind, even, mine)
        total = contract(rows_in, weight[...], 1, 1).reshape(blocks, rows, -1)
        out[:mid, :, lanes] = (total[:mid] + got_first[:, :, lanes]).astype(BF16)
        out[mid:, :, lanes] = (total[mid:] + got_second[:, :, lanes]).astype(BF16)


def middle_body(parts, out):
    units = parts.shape[2] // 3
    total = parts[0].astype(F32)
    for i in range(1, parts.shape[0]):
        total += parts[i].astype(F32)
    hid, gate_delta, up_delta = nonlinear(
        total[:, :units], total[:, units : 2 * units], total[:, 2 * units :]
    )
    row = jnp.concatenate([gate_delta, up_delta, hid], 1)
    out[...] = jnp.broadcast_to(row[None], out.shape)


def part_of(deltas, pair):
    lanes = pair.shape[0]
    rows = deltas[...].reshape(-1, deltas.shape[-1])[:, :lanes]
    return contract(rows, pair[...], 1, 0)


def part_body(deltas, pair, keep, send):
    part = part_of(deltas, pair).reshape(2 * keep.shape[0], *keep.shape[1:])
    keep[...] = part[: keep.shape[0]]
    send[...] = part[keep.shape[0] :].astype(BF16)


def add_body(where, keep_own, got_own, keep_other, got_other, _, out):
    count = keep_own.shape[0]
    for half, keep, got in ((where[0], keep_own, got_own), (1 - where[0], keep_other, got_other)):
        out[pl.ds(half * count, count)] = (keep[...] + got[...].astype(F32)).astype(BF16)


def grads_body(where, even, mine, theirs, own, other, gate_out, up_out, down_out, done):
    done[...] = jnp.zeros_like(done)
    units = gate_out.shape[0]
    deltas = [ref[...].reshape(-1, ref.shape[-1]) for ref in (own, other)]

    def total_of(kind, lanes):
        halves = ((where[0], mine), (1 - where[0], theirs))
        rows = jnp.concatenate([half_rows(h, kind, even, odd) for h, odd in halves], 0)
        return contract(jnp.concatenate([m[:, lanes] for m in deltas], 0), rows, 0, 0).astype(BF16)

    pair = total_of(0, slice(0, 2 * units))
    gate_out[...] = pair[:units]
    up_out[...] = pair[units:]
    down_out[...] = total_of(1, slice(2 * units, 3 * units))


def swap_cores(value):
    return lax.ppermute(value, "core", [(0, 1), (1, 0)])


def from_neighbour(value, by):
    pairs = [(c * 16 + (i + by[c]) % 16, c * 16 + i) for c in range(2) for i in range(16)]
    return lax.ppermute(value, ("core", "col"), pairs)


def per_device(inputs, out_grad, gate_weight, up_weight, down_weight):
    tokens, width = inputs.shape
    units = gate_weight.shape[1]
    n = 16
    half = n * tokens // 2
    where = lax.axis_index("core").astype(jnp.int32).reshape(1)
    pair = jnp.concatenate([gate_weight.T, up_weight.T], 0)

    parity = [list(range(i, n, 2)) for i in range(2)]
    both = jnp.stack([inputs, out_grad])
    even = lax.all_gather(both, "col", axis=0, axis_index_groups=parity)
    count, core = n // 4, lax.axis_index("core")
    parts_of = [lax.dynamic_slice_in_dim(even, c * count, count, 0) for c in (1 - core, core)]
    theirs, mine = from_neighbour(parts_of[0], (-1, 1)), from_neighbour(parts_of[1], (1, -1))

    flops = 2 * half * units * width
    sds = jax.ShapeDtypeStruct
    sent = sds((n // 2, half // n, 3 * units), F32)
    weights = (pair, down_weight)
    first = swap_cores(call(send_first_body, sent, 3 * flops // 2, where, even, *weights))
    second = call(send_second_body, sent, 3 * flops // 2, theirs, *weights, after=(mine,))
    second = swap_cores(second)
    parts = call(
        keep_body,
        sds((n, half // n, 3 * units), BF16),
        3 * flops,
        where,
        even,
        mine,
        *weights,
        first,
        second,
    )
    parts = lax.all_to_all(parts, XY, 0, 0)
    row = call(middle_body, sds(parts.shape, BF16), 40 * half // n * units, parts)
    own = lax.all_to_all(row, XY, 0, 0)
    other = swap_cores(own)
    some = (n // 4, tokens, width)
    outs = (sds(some, F32), sds(some, BF16))
    keep_own, send_own = call(part_body, outs, 2 * flops, own, pair)
    got_own = from_neighbour(send_own, (1, -1))
    keep_other, send_other = call(part_body, outs, 2 * flops, other, pair)
    got_other = from_neighbour(send_other, (-1, 1))
    grad = sds((units, width), BF16)
    gate_grad, up_grad, down_grad, done = call(
        grads_body,
        (grad, grad, grad, sds((8, 128), F32)),
        6 * flops,
        where,
        even,
        mine,
        theirs,
        own,
        other,
    )
    added = (keep_own, got_own, keep_other, got_other)
    pieces = call(add_body, sds((n // 2, tokens, width), BF16), 0, where, *added, after=(done,))
    pieces = lax.all_to_all(pieces, "col", 0, 0, axis_index_groups=parity)
    input_grad = jnp.sum(pieces.astype(F32), axis=0).astype(BF16)
    return (input_grad, gate_grad.T, up_grad.T, down_grad)


def solution(mesh):
    grid = Mesh(mesh.devices.reshape(4, 4, 2, 16), ("x", "y", "core", "col"))
    row = ("x", "y", "core")
    return jax.shard_map(
        per_device,
        mesh=grid,
        in_specs=(P("col", row), P("col", row), P(row, "col"), P(row, "col"), P("col", row)),
        out_specs=(P("col", row), P(row, "col"), P(row, "col"), P("col", row)),
        check_vma=False,
    )
```
